32 devices in a mesh: pp: 2 (over core), ep: 4 (over z), tp: 4 (over y, x).
Axes of the slice: x: 2, y: 2, z: 4, core: 2. Of those that a mesh axis runs over, the one named last changes fastest.
Arguments:
- tokens: bfloat16 [2, 512, 4096], P('pp', 'ep'), may hold values from -300 to 300
- routes: int32 [2, 512, 8], P('pp', 'ep'), may hold values from 0 to 63, all different within a row; in each aligned block of 32 rows (0 to 31, 32 to 63, ..., all dimensions but the last counted through in order) at most 6 rows name the same one
- gates: float32 [2, 512, 8], P('pp', 'ep'), may hold values from 0.05 to 0.5
- norm_gain: bfloat16 [2, 4096], P('pp'), may hold values from 0.099609375 to 1.8984375
- w_gate: bfloat16 [2, 64, 768, 4096], P('pp', 'ep', 'tp'), may hold values from -0.09375 to 0.09375
- w_up: bfloat16 [2, 64, 768, 4096], P('pp', 'ep', 'tp'), may hold values from -0.09375 to 0.09375
- w_down: bfloat16 [2, 64, 768, 4096], P('pp', 'ep', 'tp'), may hold values from -0.21875 to 0.21875
Outputs:
- expert_mix: bfloat16 [2, 512, 4096], P('pp', ('ep', 'tp'))
- handoff_payload: bfloat16 [2, 512, 4096], P('pp', ('ep', 'tp'))
- handoff_scale: bfloat16 [2, 512, 32], P('pp', ('ep', 'tp'))
The draws below stay inside these ranges and needn't reach their ends.
Inputs may be any that keep to these rules, and one draw needn't show every extreme that they name: `routes`: in each aligned block of 32 consecutive tokens of a section no expert is chosen more than 6 times; in some blocks one expert is chosen exactly 6 times.
All inputs are finite; a program needn't handle non-finite values. Where the reference program divides by a largest or mean magnitude, that divisor is 1e-20 or more.
Results may differ from the reference program's by a relative error of at most 0.012.
Values may be sent and summed in bfloat16 or wider, within the bound.
A program may use at most 256 MiB of HBM per device.

```python
import math
import jax
import jax.numpy as jnp
import numpy as np
from jax import lax

D = 4096
FF = 768
EXPERTS = 64
TOP = 8
BLOCK = 128
TOKENS = 512
SHARE = 32
MOST = 6
N_TP = 4


def draw_tokens(key, part):
    key = jax.random.fold_in(key, 11)
    first, second, third = jax.random.split(key, 3)
    rows = jnp.exp(jax.random.uniform(second, (2, TOKENS, 1), jnp.float32, math.log(0.5), math.log(5.0)))
    cols = jnp.exp(jax.random.uniform(third, (2, 1, D), jnp.float32, math.log(0.5), math.log(5.0)))
    base = jnp.clip(jax.random.normal(first, (2, TOKENS, D), jnp.float32), -4.0, 4.0)
    return (base * rows * cols).astype(jnp.bfloat16)


def levels(rng, dims, shards, least, high):
    def one(position, parts):
        heights = jax.random.uniform(jax.random.fold_in(jax.random.fold_in(rng, 6), position), (parts,), jnp.float32, least / len(shards), high / len(shards))
        return jnp.repeat(jnp.exp(heights), dims[position] // parts).reshape((-1,) + (1,) * (len(dims) - position - 1))

    factor_of = one(*shards[0])
    for cut in shards[1:]:
        factor_of = factor_of * one(*cut)
    return factor_of


def shared_out(rng, own, number, rows, count, top, bound, skew):
    order = jax.random.permutation(rng, count)
    heavy_load, ordinary = shares(count, rows * top, bound, skew, True), shares(count, rows * top, bound, skew, False)
    places = jnp.arange(count)

    def named(sizes, turn):
        used = int((sizes > 0).sum())
        fixed = max(1, used // 4)
        moved = fixed + (places - fixed + turn * (used - fixed)) % max(1, count - fixed)
        return jnp.zeros((count,), jnp.int32).at[order[jnp.where(places < fixed, places, moved)]].set(jnp.asarray(sizes, jnp.int32))

    sizes = jnp.where(number % 4 == 0, named(heavy_load, number // 4), named(ordinary, number - number // 4 - 1))
    mixed = jax.random.permutation(jax.random.fold_in(own, 3), count)
    donor, sink = mixed[0:count // 2 * 2:2], mixed[1:count // 2 * 2:2]
    room = jnp.minimum(sizes[donor] - 1, bound - sizes[sink]) // 2
    room = jnp.where((donor == order[0]) | (sink == order[0]) | (sizes[sink] == 0), 0, jnp.maximum(room, 0))
    moved = jax.random.randint(jax.random.fold_in(own, 4), (count // 2,), 0, 1 << 20) % (room + 1)
    sizes = sizes.at[donor].add(-moved).at[sink].add(moved)
    items = jnp.searchsorted(jnp.cumsum(sizes), jnp.arange(rows * top), side="right").astype(jnp.int32)
    listing = items.reshape(top, rows).T
    listing = listing[jax.random.permutation(jax.random.fold_in(own, 1), rows)]
    turn = jax.random.randint(jax.random.fold_in(own, 2), (rows, 1), 0, top)
    return jnp.take_along_axis(listing, (jnp.arange(top)[None, :] + turn) % top, axis=1)


def shares(amount, total, limit, lean, full):
    weights = [(1 << 20) // math.isqrt(grade ** lean) + 1 for grade in range(1, amount + 1)]
    largest = limit if full else min(limit, max(-(-total // amount), total * weights[0] // sum(weights)))
    least = 1 if total - largest >= amount - 1 else 0
    holding, rest = [largest] + [least] * (amount - 1), total - largest - least * (amount - 1)
    while rest > 0:
        movable = [i for i in range(1, amount) if holding[i] < largest] or [i for i in range(1, amount) if holding[i] < limit]
        pool, left = sum([weights[i] for i in movable]), rest
        for i in movable:
            extra = min(limit - holding[i], max(1, left * weights[i] // pool), rest)
            holding[i] = holding[i] + extra
            rest = rest - extra
    return np.array(holding)


def scatter_about(stream_key, dims, scale, bound, cuts=(), kind=jnp.bfloat16):
    level = levels(stream_key, dims, cuts, -0.22, 0.18) if cuts else 1.0
    entries = jax.random.normal(stream_key, dims, jnp.float32) * scale * level
    return jnp.minimum(jnp.maximum(entries, -bound), bound).astype(kind)


def setup_inputs(seed: int = 0) -> dict:
    key_list = jax.random.split(jax.random.key(seed), 8)
    tokens = draw_tokens(jax.random.fold_in(key_list[7], 71), 0)
    routes_keys = jax.random.split(jax.random.fold_in(key_list[1], 1), 2 * TOKENS // SHARE)
    routes_turns = jax.random.permutation(jax.random.fold_in(key_list[1], 3), 2 * TOKENS // SHARE)
    routes = jax.vmap(lambda own, number: shared_out(jax.random.fold_in(key_list[1], 2), own, number, SHARE, EXPERTS, TOP, MOST, 2))(routes_keys, routes_turns).reshape((2, TOKENS, TOP))
    gates = jnp.clip(jnp.exp(math.log(0.5) - 2.3025851 * jax.random.uniform(key_list[2], (2, TOKENS, TOP), jnp.float32) ** levels(key_list[2], (2, TOKENS, TOP), ((0, 2), (1, 4)), -0.2, 0.2)), 0.05, 0.5)
    norm_gain = jnp.clip(1.0 + 0.18 * jax.random.normal(key_list[3], (2, D), jnp.float32), 0.099609375, 1.8984375).astype(jnp.bfloat16)
    w_gate = scatter_about(key_list[4], (2, EXPERTS, FF, D), D ** -0.5, 0.09375, ((0, 2), (1, 4), (2, 4)))
    w_up = scatter_about(key_list[5], (2, EXPERTS, FF, D), D ** -0.5, 0.09375, ((0, 2), (1, 4), (2, 4)))
    w_down = scatter_about(key_list[6], (2, EXPERTS, FF, D), FF ** -0.5, 0.21875, ((0, 2), (1, 4), (2, 4)))
    return dict(tokens=tokens, routes=routes, gates=gates, norm_gain=norm_gain, w_gate=w_gate, w_up=w_up, w_down=w_down)


def slot_ids(block_routes):
    flat = block_routes.reshape(-1)
    onehot = (flat[:, None] == jnp.arange(EXPERTS, dtype=jnp.int32)[None, :]).astype(jnp.int32)
    earlier = jnp.cumsum(onehot, axis=0) - onehot
    return flat * MOST + lax.optimization_barrier(jnp.sum(earlier * onehot, axis=1))

def expert_rows(rows, gate_w, up_w, down_w):
    gate_pre = jnp.dot(rows, gate_w.T, preferred_element_type=jnp.float32)
    up_pre = jnp.dot(rows, up_w.T, preferred_element_type=jnp.float32)
    hidden = (jax.nn.silu(gate_pre) * up_pre).astype(jnp.bfloat16)
    group = FF // N_TP
    total = jnp.zeros((rows.shape[0], D), jnp.float32)
    for index in range(N_TP):
        term = jnp.dot(hidden[:, index * group:(index + 1) * group], down_w[index * group:(index + 1) * group], preferred_element_type=jnp.float32)
        rounded = lax.optimization_barrier(term.astype(jnp.bfloat16))
        total = total + rounded.astype(jnp.float32)
    return total.astype(jnp.bfloat16)

def one_section(source, section_routes, section_gates, gain, gate_w, up_w, down_w):
    x = source.astype(jnp.float32)
    normed = (x * lax.rsqrt(lax.optimization_barrier(jnp.mean(x * x, axis=1, keepdims=True)) + 1e-06) * gain.astype(jnp.float32)[None, :]).astype(jnp.bfloat16)
    blocks = TOKENS // SHARE
    slots = jax.vmap(slot_ids)(section_routes.reshape(blocks, SHARE, TOP))
    offsets = (jnp.arange(blocks, dtype=jnp.int32) * (EXPERTS * MOST))[:, None]
    target = (slots + offsets).reshape(-1)
    token_index = jnp.repeat(jnp.arange(TOKENS, dtype=jnp.int32), TOP)
    tok_table = jnp.zeros((blocks * EXPERTS * MOST,), jnp.int32).at[target].set(token_index)
    gate_table = jnp.zeros((blocks * EXPERTS * MOST,), jnp.float32).at[target].set(section_gates.reshape(-1).astype(jnp.float32))
    tok_table = tok_table.reshape(blocks, EXPERTS, MOST).transpose(1, 0, 2).reshape(EXPERTS, blocks * MOST)
    gate_table = gate_table.reshape(blocks, EXPERTS, MOST).transpose(1, 0, 2).reshape(EXPERTS, blocks * MOST)

    def per_expert(total, inputs):
        toks, weights, gate_e, up_e, down_e = inputs
        out = expert_rows(normed[toks], gate_e, up_e, down_e)
        return (total.at[toks].add(weights[:, None] * out.astype(jnp.float32)), None)
    mix, _ = lax.scan(per_expert, jnp.zeros((TOKENS, D), jnp.float32), (tok_table, gate_table, gate_w, up_w, down_w))
    full = (x + mix).reshape(TOKENS, D // BLOCK, BLOCK)
    scale = (lax.optimization_barrier(jnp.max(jnp.abs(full), axis=2)) + 1e-06).astype(jnp.bfloat16)
    payload = (full / scale.astype(jnp.float32)[:, :, None]).astype(jnp.bfloat16).reshape(TOKENS, D)
    return (mix.astype(jnp.bfloat16), payload, scale)

def reference(tokens, routes, gates, norm_gain, w_gate, w_up, w_down):
    mixes, payloads, scales = ([], [], [])
    for section in range(2):
        mix, payload, scale = one_section(tokens[section], routes[section], gates[section], norm_gain[section], w_gate[section], w_up[section], w_down[section])
        mixes.append(mix)
        payloads.append(payload)
        scales.append(scale)
    return (jnp.stack(mixes), jnp.stack([payloads[1], payloads[0]]), jnp.stack([scales[1], scales[0]]))
```

```python
import jax
import jax.numpy as jnp
from jax import lax
from jax.sharding import PartitionSpec as P

TOP = 8
BLOCK = 128
EXTRA = 128


def passed_along(value, axis, steps):
    count = lax.axis_size(axis)
    pairs = [(source, (source + steps) % count) for source in range(count)]
    return lax.ppermute(value, axis, pairs)


def per_device(tokens, routes, gates, norm_gain, w_gate, w_up, w_down):
    parts = lax.axis_size("tp")
    rank = lax.axis_index("tp")
    peers = lax.axis_size("ep")
    local = w_gate.shape[1]
    ff_part = w_gate.shape[2]
    width = tokens.shape[2]
    experts = local * peers
    share = tokens.shape[1] // parts
    total = share * parts * peers
    blocks = parts * peers
    capacity = min(share, max(2, 3 * share * TOP // (2 * experts)))
    first_expert = lax.axis_index("ep") * local

    source = lax.dynamic_slice_in_dim(tokens[0], rank * share, share, 0).astype(jnp.float32)
    inverse = lax.rsqrt(jnp.mean(source * source, axis=1, keepdims=True) + 1e-06)
    normed = (source * inverse * norm_gain[0].astype(jnp.float32)[None, :]).astype(jnp.bfloat16)
    my_routes = lax.dynamic_slice_in_dim(routes[0], rank * share, share, 0)
    my_gates = lax.dynamic_slice_in_dim(gates[0], rank * share, share, 0)
    small = jnp.concatenate([my_routes.astype(jnp.float32), my_gates], axis=1)
    small_all = lax.all_gather(small, ("ep", "tp"), axis=0, tiled=True)
    rows_all = lax.all_gather(normed, ("ep", "tp"), axis=0, tiled=True)

    route_all = small_all[:, :TOP].astype(jnp.int32)
    gate_all = small_all[:, TOP:]
    mine = first_expert + jnp.arange(local, dtype=jnp.int32)
    match = route_all[:, :, None] == mine[None, None, :]
    chosen = jnp.any(match, axis=1)
    weight = jnp.sum(jnp.where(match, gate_all[:, :, None], 0.0), axis=1)
    counted = chosen.astype(jnp.int32).reshape(blocks, share, local)
    earlier = (jnp.cumsum(counted, axis=1) - counted).reshape(total, local)
    base = (jnp.arange(total, dtype=jnp.int32) // share * capacity)[:, None]
    slot = jnp.where(chosen, base + earlier, -1)
    table = (
        slot.T[:, None, :] == jnp.arange(blocks * capacity, dtype=jnp.int32)[None, :, None]
    )
    table16 = table.astype(jnp.bfloat16)
    slot_gate = jnp.sum(jnp.where(table, weight.T[:, None, :], 0.0), axis=2)
    rows = jnp.einsum("lst,td->lsd", table16, rows_all, preferred_element_type=jnp.float32)
    rows = rows.astype(jnp.bfloat16)
    gate_pre = jnp.einsum("lsd,lfd->lsf", rows, w_gate[0], preferred_element_type=jnp.float32)
    up_pre = jnp.einsum("lsd,lfd->lsf", rows, w_up[0], preferred_element_type=jnp.float32)
    hidden = (jax.nn.silu(gate_pre) * up_pre * slot_gate[:, :, None]).astype(jnp.bfloat16)
    spread = jnp.einsum("lst,lsf->tlf", table16, hidden, preferred_element_type=jnp.float32)
    spread = spread.astype(jnp.bfloat16).reshape(total, local * ff_part)
    part = jnp.dot(
        spread, w_down[0].reshape(local * ff_part, width), preferred_element_type=jnp.float32
    ).astype(jnp.bfloat16)
    mixed = lax.psum_scatter(part, ("ep", "tp"), scatter_dimension=0, tiled=True)
    mixed = mixed.astype(jnp.float32)
    full = source + mixed
    blocked = full.reshape(share, width // BLOCK, BLOCK)
    scale = (jnp.max(jnp.abs(blocked), axis=2) + 1e-06).astype(jnp.bfloat16)
    payload = (
        (blocked / scale.astype(jnp.float32)[:, :, None]).astype(jnp.bfloat16).reshape(share, width)
    )
    payload_in, scale_in = passed_along((payload, scale), "pp", 1)
    return (mixed.astype(jnp.bfloat16)[None], payload_in[None], scale_in[None])


def solution(mesh):
    return jax.shard_map(
        per_device,
        mesh=mesh,
        in_specs=(
            P("pp", "ep", None),
            P("pp", "ep", None),
            P("pp", "ep", None),
            P("pp", None),
            P("pp", "ep", "tp", None),
            P("pp", "ep", "tp", None),
            P("pp", "ep", "tp", None),
        ),
        out_specs=(
            P("pp", ("ep", "tp"), None),
            P("pp", ("ep", "tp"), None),
            P("pp", ("ep", "tp"), None),
        ),
        check_vma=False,
    )
```

```python
import functools

import jax
import jax.numpy as jnp
from jax import lax
from jax.experimental import pallas as pl
from jax.experimental.pallas import tpu as pltpu
from jax.sharding import PartitionSpec as P

TOP = 8
BLOCK = 128
EXTRA = 128
CHUNK = 512
PAIR = 2
LAG = 2
MESH = pl.DeviceIdType.MESH


def passed_along(value, axis, steps):
    count = lax.axis_size(axis)
    pairs = [(source, (source + steps) % count) for source in range(count)]
    return lax.ppermute(value, axis, pairs)


def hidden_kernel(width, slots, rows_ref, slot_row_ref, weight_row_ref, slot_col_ref, gate_ref, up_ref, out_ref):
    step = pl.program_id(0)
    group, _, total = slot_row_ref.shape
    ff_part = gate_ref.shape[1]
    tables = []
    scales = []
    for i in range(group):
        hit = lax.broadcasted_iota(jnp.int32, (slots, total), 0) == slot_row_ref[i]
        tables.append(hit.astype(jnp.float32).astype(jnp.bfloat16))
        scales.append(jnp.sum(jnp.where(hit, weight_row_ref[i], 0.0), axis=1, keepdims=True))
    rows = jnp.dot(
        jnp.concatenate(tables, axis=0), rows_ref[:, :width], preferred_element_type=jnp.float32
    ).astype(jnp.bfloat16)
    contract = (((1,), (1,)), ((), ()))
    slot_col = slot_col_ref[...]
    lane = lax.broadcasted_iota(jnp.int32, slot_col.shape, 1)
    for i in range(group):
        mine = rows[i * slots:(i + 1) * slots]
        gate_pre = lax.dot_general(mine, gate_ref[i], contract, preferred_element_type=jnp.float32)
        up_pre = lax.dot_general(mine, up_ref[i], contract, preferred_element_type=jnp.float32)
        hidden = gate_pre / (1.0 + jnp.exp(-gate_pre)) * up_pre * scales[i]
        column = jnp.sum(
            jnp.where(lane == step * group + i, slot_col, 0), axis=1, keepdims=True
        )
        back = lax.broadcasted_iota(jnp.int32, (total, slots), 1) == column
        spread = jnp.dot(
            back.astype(jnp.float32).astype(jnp.bfloat16),
            hidden.astype(jnp.bfloat16),
            preferred_element_type=jnp.float32,
        )
        out_ref[:, i * ff_part:(i + 1) * ff_part] = spread.astype(jnp.bfloat16)


def hidden_spread(rows_all, slot, weight, slot_out, w_gate, w_up, slots):
    total, local = slot.shape
    ff_part, width = w_gate.shape[1:]
    return pl.pallas_call(
        functools.partial(hidden_kernel, width, slots),
        out_shape=jax.ShapeDtypeStruct((total, local * ff_part), jnp.bfloat16),
        grid=(local // PAIR,),
        in_specs=[
            pl.BlockSpec(rows_all.shape, lambda i: (0, 0)),
            pl.BlockSpec((PAIR, 1, total), lambda i: (i, 0, 0)),
            pl.BlockSpec((PAIR, 1, total), lambda i: (i, 0, 0)),
            pl.BlockSpec((total, local), lambda i: (0, 0)),
            pl.BlockSpec((PAIR, ff_part, width), lambda i: (i, 0, 0)),
            pl.BlockSpec((PAIR, ff_part, width), lambda i: (i, 0, 0)),
        ],
        out_specs=pl.BlockSpec((total, PAIR * ff_part), lambda i: (0, i)),
        compiler_params=pltpu.CompilerParams(vmem_limit_bytes=50 * 2**20),
        name="hidden_spread",
    )(rows_all, slot.T[:, None, :], weight.T[:, None, :], slot_out, w_gate, w_up)


def down_kernel(groups, peers, spread_ref, w_ref, out_ref, w_buf, send1, recv1, send2, recv2, w_sem, s1, r1, s2, r2):
    chunks = send1.shape[0]
    group_rows = send2.shape[1]
    block_rows = recv2.shape[2]
    me_tp = lax.axis_index("tp")
    me_ep = lax.axis_index("ep")

    def load(c):
        slot = lax.rem(c, 3)
        columns = pl.ds(pl.multiple_of(c * CHUNK, CHUNK), CHUNK)
        return pltpu.make_async_copy(w_ref.at[:, columns], w_buf.at[slot], w_sem.at[slot])

    def first(c, k):
        peer = lax.rem(me_tp + k, groups)
        return pltpu.make_async_remote_copy(
            src_ref=send1.at[c, pl.ds(pl.multiple_of(peer * group_rows, group_rows), group_rows)],
            dst_ref=recv1.at[c, k - 1],
            send_sem=s1.at[c, k - 1],
            recv_sem=r1.at[c, k - 1],
            device_id={"tp": peer},
            device_id_type=MESH,
        )

    def second(c, k):
        peer = lax.rem(me_ep + k, peers)
        return pltpu.make_async_remote_copy(
            src_ref=send2.at[c, pl.ds(pl.multiple_of(peer * block_rows, block_rows), block_rows)],
            dst_ref=recv2.at[c, k - 1],
            send_sem=s2.at[c, k - 1],
            recv_sem=r2.at[c, k - 1],
            device_id={"ep": peer},
            device_id_type=MESH,
        )

    load(0).start()
    load(1).start()
    barrier = pltpu.get_barrier_semaphore()
    for k in range(1, groups):
        pl.semaphore_signal(
            barrier, inc=1, device_id={"tp": lax.rem(me_tp + k, groups)}, device_id_type=MESH
        )
    for k in range(1, peers):
        pl.semaphore_signal(
            barrier, inc=1, device_id={"ep": lax.rem(me_ep + k, peers)}, device_id_type=MESH
        )
    pl.semaphore_wait(barrier, groups + peers - 2)

    def step(c, carry):
        @pl.when(c < chunks)
        def _():
            load(c).wait()

            @pl.when(c + 2 < chunks)
            def _():
                load(c + 2).start()

            send1[c] = jnp.dot(
                spread_ref[...], w_buf[lax.rem(c, 3)], preferred_element_type=jnp.float32
            ).astype(jnp.bfloat16)
            for k in range(1, groups):
                first(c, k).start()

        @pl.when((c >= LAG) & (c < chunks + LAG))
        def _():
            d = c - LAG
            own = pl.ds(pl.multiple_of(me_tp * group_rows, group_rows), group_rows)
            value = send1[d, own].astype(jnp.float32)
            for k in range(1, groups):
                first(d, k).wait_recv()
                value = value + recv1[d, k - 1].astype(jnp.float32)
            send2[d] = value.astype(jnp.bfloat16)
            for k in range(1, peers):
                second(d, k).start()

        @pl.when(c >= 2 * LAG)
        def _():
            d = c - 2 * LAG
            own = pl.ds(pl.multiple_of(me_ep * block_rows, block_rows), block_rows)
            value = send2[d, own].astype(jnp.float32)
            for k in range(1, peers):
                second(d, k).wait_recv()
                value = value + recv2[d, k - 1].astype(jnp.float32)
            out_ref[:, pl.ds(pl.multiple_of(d * CHUNK, CHUNK), CHUNK)] = value

        return carry

    lax.fori_loop(0, chunks + 2 * LAG, step, 0)

    def drain(c, carry):
        for k in range(1, groups):
            first(c, k).wait_send()
        for k in range(1, peers):
            second(c, k).wait_send()
        return carry

    lax.fori_loop(0, chunks, drain, 0)


def down_scatter(spread, w_down, groups, peers):
    total, depth = spread.shape
    width = w_down.shape[1]
    chunks = width // CHUNK
    group_rows = total // groups
    block_rows = group_rows // peers
    return pl.pallas_call(
        functools.partial(down_kernel, groups, peers),
        out_shape=jax.ShapeDtypeStruct((block_rows, width), jnp.float32),
        in_specs=[pl.BlockSpec(memory_space=pltpu.VMEM), pl.BlockSpec(memory_space=pl.ANY)],
        out_specs=pl.BlockSpec(memory_space=pltpu.VMEM),
        scratch_shapes=[
            pltpu.VMEM((3, depth, CHUNK), jnp.bfloat16),
            pltpu.VMEM((chunks, total, CHUNK), jnp.bfloat16),
            pltpu.VMEM((chunks, groups - 1, group_rows, CHUNK), jnp.bfloat16),
            pltpu.VMEM((chunks, group_rows, CHUNK), jnp.bfloat16),
            pltpu.VMEM((chunks, peers - 1, block_rows, CHUNK), jnp.bfloat16),
            pltpu.SemaphoreType.DMA((3,)),
            pltpu.SemaphoreType.DMA((chunks, groups - 1)),
            pltpu.SemaphoreType.DMA((chunks, groups - 1)),
            pltpu.SemaphoreType.DMA((chunks, peers - 1)),
            pltpu.SemaphoreType.DMA((chunks, peers - 1)),
        ],
        compiler_params=pltpu.CompilerParams(
            collective_id=0, has_side_effects=True, vmem_limit_bytes=50 * 2**20
        ),
        name="down_scatter",
    )(spread, w_down)


def per_device(tokens, routes, gates, norm_gain, w_gate, w_up, w_down):
    parts = lax.axis_size("tp")
    rank = lax.axis_index("tp")
    peers = lax.axis_size("ep")
    local = w_gate.shape[1]
    ff_part = w_gate.shape[2]
    width = tokens.shape[2]
    experts = local * peers
    share = tokens.shape[1] // parts
    total = share * parts * peers
    blocks = parts * peers
    capacity = min(share, max(2, 3 * share * TOP // (2 * experts)))
    first_expert = lax.axis_index("ep") * local

    source = lax.dynamic_slice_in_dim(tokens[0], rank * share, share, 0).astype(jnp.float32)
    inverse = lax.rsqrt(jnp.mean(source * source, axis=1, keepdims=True) + 1e-06)
    normed = (source * inverse * norm_gain[0].astype(jnp.float32)[None, :]).astype(jnp.bfloat16)
    my_routes = lax.dynamic_slice_in_dim(routes[0], rank * share, share, 0)
    my_gates = lax.dynamic_slice_in_dim(gates[0], rank * share, share, 0)
    gate_high = lax.reduce_precision(my_gates, 8, 7)
    small = jnp.concatenate(
        [
            my_routes.astype(jnp.bfloat16),
            gate_high.astype(jnp.bfloat16),
            (my_gates - gate_high).astype(jnp.bfloat16),
            jnp.zeros((share, EXTRA - 3 * TOP), jnp.bfloat16),
        ],
        axis=1,
    )
    packed = jnp.concatenate([normed, small], axis=1)
    rows_all = lax.all_gather(packed, ("ep", "tp"), axis=0, tiled=True)
    small_all = rows_all[:, width:width + 3 * TOP].astype(jnp.float32)
    route_all = small_all[:, :TOP].astype(jnp.int32)
    gate_all = small_all[:, TOP:2 * TOP] + small_all[:, 2 * TOP:]
    mine = first_expert + jnp.arange(local, dtype=jnp.int32)
    match = route_all[:, :, None] == mine[None, None, :]
    chosen = jnp.any(match, axis=1)
    weight = jnp.sum(jnp.where(match, gate_all[:, :, None], 0.0), axis=1)
    counted = chosen.astype(jnp.int32).reshape(blocks, share, local)
    earlier = (jnp.cumsum(counted, axis=1) - counted).reshape(total, local)
    base = (jnp.arange(total, dtype=jnp.int32) // share * capacity)[:, None]
    slot = jnp.where(chosen, base + earlier, -1)
    if total * width <= 2**22 and local % PAIR == 0 and width % CHUNK == 0:
        slot_out = slot.reshape(peers, parts, share, local).swapaxes(0, 1).reshape(total, local)
        spread = hidden_spread(
            rows_all, slot, weight, slot_out, w_gate[0], w_up[0], blocks * capacity
        )
        mixed = down_scatter(spread, w_down[0].reshape(local * ff_part, width), parts, peers)
    else:
        table = (
            slot.T[:, None, :] == jnp.arange(blocks * capacity, dtype=jnp.int32)[None, :, None]
        )
        table16 = table.astype(jnp.bfloat16)
        slot_gate = jnp.sum(jnp.where(table, weight.T[:, None, :], 0.0), axis=2)
        rows = jnp.einsum("lst,td->lsd", table16, rows_all[:, :width], preferred_element_type=jnp.float32)
        rows = rows.astype(jnp.bfloat16)
        gate_pre = jnp.einsum("lsd,lfd->lsf", rows, w_gate[0], preferred_element_type=jnp.float32)
        up_pre = jnp.einsum("lsd,lfd->lsf", rows, w_up[0], preferred_element_type=jnp.float32)
        hidden = (jax.nn.silu(gate_pre) * up_pre * slot_gate[:, :, None]).astype(jnp.bfloat16)
        spread = jnp.einsum("lst,lsf->tlf", table16, hidden, preferred_element_type=jnp.float32)
        spread = spread.astype(jnp.bfloat16).reshape(total, local * ff_part)
        part = jnp.dot(
            spread, w_down[0].reshape(local * ff_part, width), preferred_element_type=jnp.float32
        ).astype(jnp.bfloat16)
        mixed = lax.psum_scatter(part, ("ep", "tp"), scatter_dimension=0, tiled=True)
    mixed = mixed.astype(jnp.float32)
    full = source + mixed
    blocked = full.reshape(share, width // BLOCK, BLOCK)
    scale = (jnp.max(jnp.abs(blocked), axis=2) + 1e-06).astype(jnp.bfloat16)
    payload = (
        (blocked / scale.astype(jnp.float32)[:, :, None]).astype(jnp.bfloat16).reshape(share, width)
    )
    payload_in, scale_in = passed_along((payload, scale), "pp", 1)
    return (mixed.astype(jnp.bfloat16)[None], payload_in[None], scale_in[None])


def solution(mesh):
    return jax.shard_map(
        per_device,
        mesh=mesh,
        in_specs=(
            P("pp", "ep", None),
            P("pp", "ep", None),
            P("pp", "ep", None),
            P("pp", None),
            P("pp", "ep", "tp", None),
            P("pp", "ep", "tp", None),
            P("pp", "ep", "tp", None),
        ),
        out_specs=(
            P("pp", ("ep", "tp"), None),
            P("pp", ("ep", "tp"), None),
            P("pp", ("ep", "tp"), None),
        ),
        check_vma=False,
    )
```
